32 devices in a mesh: cells: 8 (over z, y), sub: 4 (over x, core).
Axes of the slice: x: 2, y: 2, z: 4, core: 2. Of those that a mesh axis runs over, the one named last changes fastest.
Arguments:
- leaf_multipoles: bfloat16 [32768, 296], P(('cells', 'sub')), may hold values from -6 to 6
- occupancy: int32 [32768], P(('cells', 'sub')), may hold values 0 or 1
- upward_maps: bfloat16 [2368, 296], replicated, may hold values from -0.125 to 0.125
- transfer_maps: bfloat16 [9472, 296], replicated, may hold values from -0.125 to 0.125
- downward_maps: bfloat16 [296, 2368], replicated, may hold values from -0.375 to 0.375
- sources_seven: int32 [32768, 8], P(('cells', 'sub')), may hold values from 0 to 32767, as said below
- classes_seven: int32 [32768, 8], P(('cells', 'sub')), may hold values from 0 to 31
- sources_six: int32 [4096, 8], P(('cells', 'sub')), may hold values from 0 to 4095, as said below
- classes_six: int32 [4096, 8], P(('cells', 'sub')), may hold values from 0 to 31
- sources_five: int32 [512, 8], P(('cells', 'sub')), may hold values from 0 to 511
- classes_five: int32 [512, 8], P(('cells', 'sub')), may hold values from 0 to 31
- sources_four: int32 [64, 8], P(('cells', 'sub')), may hold values from 0 to 63
- classes_four: int32 [64, 8], P(('cells', 'sub')), may hold values from 0 to 31
Outputs:
- leaf_locals: bfloat16 [32768, 296], P(('cells', 'sub'))
The draws below stay inside these ranges and needn't reach their ends.
Inputs may be any that keep to these rules, and one draw needn't show every extreme that they name: `sources_seven`: each entry lies within half of 1024 positions of its own cell's index. `sources_six`: each entry lies within half of 128 positions of its own cell's index.
All inputs are finite; a program needn't handle non-finite values. No bound on the sum of `occupancy` on one device may be relied on, other than what follows from the above.
Results may differ from the reference program's by a relative error of at most 0.015.
Values may be sent and summed in bfloat16 or wider, within the bound.
A program may use at most 128 MiB of HBM per device.

```python
import jax
import jax.numpy as jnp
from jax import lax

COEF = 296
CLASSES = 32
LIST = 8
LEAF_DEV = 1024
L6_DEV = 128
L7_ALL = 32768
L6_ALL = 4096
L5_ALL = 512
L4_ALL = 64


def near_lists(key, count, reach):
    first_key, second_key = jax.random.split(key)
    target = jnp.arange(count, dtype=jnp.int32)[:, None]
    magnitude = jax.random.randint(first_key, (count, LIST), 1, reach + 1, dtype=jnp.int32)
    direction = jax.random.randint(second_key, (count, LIST), 0, 2, dtype=jnp.int32) * 2 - 1
    return jnp.clip(target + direction * magnitude, 0, count - 1).astype(jnp.int32)


def draw_sources_seven(key, part):
    key = jax.random.fold_in(key, 7)
    return near_lists(key, L7_ALL, LEAF_DEV // 2)


def draw_sources_six(key, part):
    key = jax.random.fold_in(key, 6)
    return near_lists(key, L6_ALL, L6_DEV // 2)


def place_ends(values, key, least, top_value):
    dims = values.shape
    spot = [jax.random.randint(jax.random.fold_in(key, axis), (), 0, dims[axis]) for axis in range(len(dims))]
    values = values.at[tuple(spot)].set(least)
    longest = dims.index(max(dims))
    spot[longest] = (spot[longest] + 1) % dims[longest]
    return values.at[tuple(spot)].set(top_value)


def block_levels(stream_key, extent, shards, low, largest):
    gain = 1.0
    for dim, blocks in shards:
        draws = jax.random.uniform(jax.random.fold_in(jax.random.fold_in(stream_key, 6), dim), (blocks,), jnp.float32, low / len(shards), largest / len(shards))
        gain = gain * jnp.repeat(jnp.exp(draws), extent[dim] // blocks).reshape((-1,) + (1,) * (len(extent) - 1 - dim))
    return gain


def noise(own_key, extent, scale, bound, shards=(), held_as=jnp.bfloat16):
    entries = jax.random.normal(own_key, extent, jnp.float32) * scale
    if len(shards) > 0:
        entries = block_levels(own_key, extent, shards, -0.22, 0.18) * entries
    return jnp.clip(entries, min=-bound, max=bound).astype(held_as)


def setup_inputs(seed: int = 0) -> dict:
    streams_of = jax.random.split(jax.random.key(seed), 14)
    leaf_multipoles = noise(streams_of[0], (L7_ALL, COEF), 1.0, 6.0, ((0, 32),))
    occupancy = place_ends((jax.random.randint(streams_of[1], (L7_ALL,), 0, 4) < 3).astype(jnp.int32), jax.random.fold_in(streams_of[1], 1), 0, 1)
    upward_maps = noise(streams_of[2], (8 * COEF, COEF), (8 * COEF) ** -0.5, 0.125)
    transfer_maps = noise(streams_of[3], (CLASSES * COEF, COEF), (LIST * COEF) ** -0.5, 0.125)
    downward_maps = noise(streams_of[4], (COEF, 8 * COEF), COEF ** -0.5, 0.375)
    sources_seven = draw_sources_seven(jax.random.fold_in(streams_of[13], 71), 0)
    classes_seven = place_ends(jax.random.randint(streams_of[6], (L7_ALL, LIST), 0, CLASSES), jax.random.fold_in(streams_of[6], 1), 0, CLASSES - 1).astype(jnp.int32)
    sources_six = draw_sources_six(jax.random.fold_in(streams_of[13], 71), 0)
    classes_six = place_ends(jax.random.randint(streams_of[8], (L6_ALL, LIST), 0, CLASSES), jax.random.fold_in(streams_of[8], 1), 0, CLASSES - 1).astype(jnp.int32)
    sources_five = place_ends(jax.random.randint(streams_of[9], (L5_ALL, LIST), 0, L5_ALL), jax.random.fold_in(streams_of[9], 1), 0, L5_ALL - 1).astype(jnp.int32)
    classes_five = place_ends(jax.random.randint(streams_of[10], (L5_ALL, LIST), 0, CLASSES), jax.random.fold_in(streams_of[10], 1), 0, CLASSES - 1).astype(jnp.int32)
    sources_four = place_ends(jax.random.randint(streams_of[11], (L4_ALL, LIST), 0, L4_ALL), jax.random.fold_in(streams_of[11], 1), 0, L4_ALL - 1).astype(jnp.int32)
    classes_four = place_ends(jax.random.randint(streams_of[12], (L4_ALL, LIST), 0, CLASSES), jax.random.fold_in(streams_of[12], 1), 0, CLASSES - 1).astype(jnp.int32)
    return dict(leaf_multipoles=leaf_multipoles, occupancy=occupancy, upward_maps=upward_maps, transfer_maps=transfer_maps, downward_maps=downward_maps, sources_seven=sources_seven, classes_seven=classes_seven, sources_six=sources_six, classes_six=classes_six, sources_five=sources_five, classes_five=classes_five, sources_four=sources_four, classes_four=classes_four)


def ascend(children, upward_maps):
    width = children.shape[1]
    merged = children.reshape(-1, 8 * width)
    return jnp.dot(merged, upward_maps, preferred_element_type=jnp.float32).astype(jnp.bfloat16)


def descend(parents, downward_maps):
    width = parents.shape[1]
    spread = jnp.dot(parents, downward_maps, preferred_element_type=jnp.float32)
    return spread.reshape(-1, width)


def far_field(multi, sources, classes, transfer_maps):
    count = sources.shape[0]
    width = multi.shape[1]
    kinds = transfer_maps.shape[0] // width
    blocked = min(count, 512)

    def one_block(pair):
        src_rows, class_rows = pair
        picked = jnp.take(multi, src_rows, axis=0).astype(jnp.float32)
        onehot = (class_rows[:, :, None] == jnp.arange(kinds, dtype=jnp.int32)[None, None, :]).astype(jnp.float32)
        grouped = jnp.einsum('tjc,tjk->tck', onehot, picked, preferred_element_type=jnp.float32)
        grouped = grouped.astype(jnp.bfloat16).reshape(blocked, kinds * width)
        return jnp.dot(grouped, transfer_maps, preferred_element_type=jnp.float32)

    result = lax.map(one_block, (sources.reshape(-1, blocked, sources.shape[1]), classes.reshape(-1, blocked, classes.shape[1])))
    return result.reshape(count, width)


def reference(leaf_multipoles, occupancy, upward_maps, transfer_maps, downward_maps, sources_seven, classes_seven, sources_six, classes_six, sources_five, classes_five, sources_four, classes_four):
    multi_seven = jnp.where(occupancy[:, None] > 0, leaf_multipoles, jnp.zeros_like(leaf_multipoles))
    multi_six = ascend(multi_seven, upward_maps)
    multi_five = ascend(multi_six, upward_maps)
    multi_four = ascend(multi_five, upward_maps)
    local_four = far_field(multi_four, sources_four, classes_four, transfer_maps).astype(jnp.bfloat16)
    local_five = (descend(local_four, downward_maps) + far_field(multi_five, sources_five, classes_five, transfer_maps)).astype(jnp.bfloat16)
    local_six = (descend(local_five, downward_maps) + far_field(multi_six, sources_six, classes_six, transfer_maps)).astype(jnp.bfloat16)
    local_seven = (descend(local_six, downward_maps) + far_field(multi_seven, sources_seven, classes_seven, transfer_maps)).astype(jnp.bfloat16)
    return local_seven
```

```python
import functools

import jax
import jax.numpy as jnp
from jax import lax
from jax.experimental import pallas as pl
from jax.experimental.pallas import tpu as pltpu
from jax.sharding import PartitionSpec as P

AXES = ("cells", "sub")
TILE = 256
VMEM_BYTES = 56 * 1024 * 1024


def shifted(value, axis, steps):
    count = lax.axis_size(axis)
    first, last = (max(0, -steps), min(count, count - steps))
    return lax.ppermute(value, axis, [(source, source + steps) for source in range(first, last)])


def ascend(children, upward_maps):
    width = children.shape[1]
    merged = children.reshape(-1, 8 * width)
    return jnp.dot(merged, upward_maps, preferred_element_type=jnp.float32).astype(jnp.bfloat16)


def gather_groups(table, base, index_ref, class_ref, picked, grouped, padded, kinds):
    width = table.shape[0]
    reach = table.shape[1]
    entries = index_ref.shape[0]
    tile = index_ref.shape[1]
    place = lax.broadcasted_iota(jnp.int32, (reach, tile), 0).astype(jnp.int16)
    for j in range(entries):
        index = (index_ref[j : j + 1, :] - base).astype(jnp.int16)
        hot = jnp.where(place == index, jnp.bfloat16(1), jnp.bfloat16(0))
        picked[j] = jnp.dot(table, hot, preferred_element_type=jnp.float32).astype(jnp.bfloat16)
    classes = class_ref[...]
    for j in range(entries - 1, 0, -1):
        total = picked[j].astype(jnp.float32)
        for i in range(j):
            same = classes[i : i + 1, :] == classes[j : j + 1, :]
            total = total + jnp.where(same, picked[i].astype(jnp.float32), 0.0)
        picked[j] = total.astype(jnp.bfloat16)
    small = classes.astype(jnp.int16)

    @pl.loop(0, kinds)
    def _(kind):
        label = kind.astype(jnp.int16)
        value = jnp.zeros((width, tile), jnp.bfloat16)
        for j in range(entries):
            value = jnp.where(small[j : j + 1, :] == label, picked[j], value)
        grouped[pl.ds(pl.multiple_of(kind * padded, 16), width), :] = value


def near_kernel(
    below_ref, own_ref, above_ref, index_ref, class_ref, maps_ref, out_ref, window, picked, grouped, *, kinds
):
    step = pl.program_id(0)
    half = below_ref.shape[0]
    count = own_ref.shape[0]
    tile = index_ref.shape[1]
    padded = grouped.shape[0] // kinds
    reach = tile + 2 * half

    @pl.when(step == 0)
    def _():
        grouped[...] = jnp.zeros_like(grouped)
        window[:, 0:half] = below_ref[...].T
        window[:, half : half + count] = own_ref[...].T
        window[:, half + count :] = above_ref[...].T

    first = pl.multiple_of(step * tile, tile)
    table = window[:, pl.ds(first, reach)]
    gather_groups(table, first, index_ref, class_ref, picked, grouped, padded, kinds)
    far = jnp.dot(maps_ref[...], grouped[...], preferred_element_type=jnp.float32)
    out_ref[...] = far.T


def near_far(below, own, above, index, classes, maps, kinds):
    count, width = own.shape
    half = below.shape[0]
    entries = index.shape[0]
    tile = min(count, TILE)
    total = maps.shape[1]
    whole = lambda shape: pl.BlockSpec(shape, lambda i: (0, 0))
    return pl.pallas_call(
        functools.partial(near_kernel, kinds=kinds),
        grid=(count // tile,),
        in_specs=[
            whole(below.shape),
            whole(own.shape),
            whole(above.shape),
            pl.BlockSpec((entries, tile), lambda i: (0, i)),
            pl.BlockSpec((entries, tile), lambda i: (0, i)),
            whole(maps.shape),
        ],
        out_specs=pl.BlockSpec((tile, width), lambda i: (i, 0)),
        out_shape=jax.ShapeDtypeStruct((count, width), jnp.float32),
        scratch_shapes=[
            pltpu.VMEM((width, count + 2 * half), jnp.bfloat16),
            pltpu.VMEM((entries, width, tile), jnp.bfloat16),
            pltpu.VMEM((total, tile), jnp.bfloat16),
        ],
        compiler_params=pltpu.CompilerParams(vmem_limit_bytes=VMEM_BYTES),
        cost_estimate=pl.CostEstimate(
            flops=2 * count * width * (total + entries * (tile + 2 * half)),
            bytes_accessed=2 * width * total,
            transcendentals=0,
        ),
    )(below, own, above, index, classes, maps)


def far_kernel(
    table_ref, index_ref, class_ref, maps_ref, down_ref, near_ref, out_ref,
    picked, grouped, far, local_five, local_six, local_seven, *, kinds, counts
):
    count_six, count_five, count_four = counts
    padded = grouped.shape[0] // kinds
    grouped[...] = jnp.zeros_like(grouped)
    gather_groups(table_ref[...], 0, index_ref, class_ref, picked, grouped, padded, kinds)
    far[...] = jnp.dot(maps_ref[...], grouped[...], preferred_element_type=jnp.float32).T
    start_four = count_six + count_five

    def descend(parents, local):
        for octant in range(8):
            spread = jnp.dot(parents, down_ref[octant], preferred_element_type=jnp.float32)
            local[:, octant, :] = spread[: local.shape[0]]
        count, _, width = local.shape
        return local[...].reshape(8 * count, width)

    rows_four = far[start_four : start_four + 16, :].astype(jnp.bfloat16)
    five = descend(rows_four, local_five) + far[count_six:start_four, :]
    six = descend(five.astype(jnp.bfloat16), local_six) + far[0:count_six, :]
    seven = descend(six.astype(jnp.bfloat16), local_seven) + near_ref[...]
    out_ref[...] = seven.astype(jnp.bfloat16)


def coarse_far(table, index, classes, maps, down, near, kinds, counts):
    width = table.shape[0]
    entries, tile = index.shape
    total = maps.shape[1]
    return pl.pallas_call(
        functools.partial(far_kernel, kinds=kinds, counts=counts),
        out_shape=jax.ShapeDtypeStruct(near.shape, jnp.bfloat16),
        scratch_shapes=[
            pltpu.VMEM((entries, width, tile), jnp.bfloat16),
            pltpu.VMEM((total, tile), jnp.bfloat16),
            pltpu.VMEM((tile, width), jnp.float32),
            pltpu.VMEM((counts[2], 8, width), jnp.float32),
            pltpu.VMEM((counts[1], 8, width), jnp.float32),
            pltpu.VMEM((counts[0], 8, width), jnp.float32),
        ],
        compiler_params=pltpu.CompilerParams(vmem_limit_bytes=VMEM_BYTES),
        cost_estimate=pl.CostEstimate(
            flops=2 * tile * width * total, bytes_accessed=2 * width * total, transcendentals=0
        ),
    )(table, index, classes, maps, down, near)


def body(
    leaf_multipoles,
    occupancy,
    upward_maps,
    transfer_maps,
    downward_maps,
    sources_seven,
    classes_seven,
    sources_six,
    classes_six,
    sources_five,
    classes_five,
    sources_four,
    classes_four,
):
    width = leaf_multipoles.shape[1]
    kinds = transfer_maps.shape[0] // width
    padded = (width + 15) // 16 * 16
    place = lax.axis_index(AXES)
    count_seven = sources_seven.shape[0]
    count_six = sources_six.shape[0]
    count_five = sources_five.shape[0]
    count_four = sources_four.shape[0]
    half = count_seven // 2

    multi_seven = jnp.where(
        occupancy[:, None] > 0, leaf_multipoles, jnp.zeros_like(leaf_multipoles)
    )
    below = shifted(multi_seven[-half:], AXES, 1)
    above = shifted(multi_seven[:half], AXES, -1)
    multi_six = ascend(multi_seven, upward_maps)
    multi_five = ascend(multi_six, upward_maps)
    table_five = lax.all_gather(multi_five, AXES, axis=0, tiled=True)

    maps = jnp.pad(
        transfer_maps.reshape(kinds, width, width), ((0, 0), (0, padded - width), (0, 0))
    ).reshape(kinds * padded, width).T
    down = downward_maps.reshape(width, 8, width).transpose(1, 0, 2)

    index_seven = (sources_seven - (place * count_seven - half)).T
    near = near_far(below, multi_seven, above, index_seven, classes_seven.T, maps, kinds)

    edges = ascend(jnp.concatenate([below, above], axis=0), upward_maps)
    reach = half // 8
    table_four = ascend(table_five, upward_maps)
    table = jnp.concatenate(
        [edges[:reach], multi_six, edges[reach:], table_five, table_four], axis=0
    )
    start_five = count_six + 2 * reach
    start_four = start_five + table_five.shape[0]
    rest = (-table.shape[0]) % 128
    table = jnp.pad(table, ((0, rest), (0, 0)))
    used = count_six + count_five + count_four
    tile = (used + 16 + 127) // 128 * 128
    index = jnp.concatenate(
        [
            sources_six - (place * count_six - reach),
            sources_five + start_five,
            sources_four + start_four,
        ],
        axis=0,
    )
    index = jnp.pad(index, ((0, tile - used), (0, 0)))
    classes = jnp.concatenate([classes_six, classes_five, classes_four], axis=0)
    classes = jnp.pad(classes, ((0, tile - used), (0, 0)), constant_values=kinds)
    return coarse_far(
        table.T, index.T, classes.T, maps, down, near, kinds, (count_six, count_five, count_four)
    )


def solution(mesh):
    row = P(AXES, None)
    in_specs = (row, P(AXES), P(), P(), P()) + (row,) * 8
    return jax.shard_map(body, mesh=mesh, in_specs=in_specs, out_specs=row, check_vma=False)
```

```python
import functools

import jax
import jax.numpy as jnp
from jax import lax
from jax.experimental import pallas as pl
from jax.experimental.pallas import tpu as pltpu
from jax.sharding import PartitionSpec as P

AXES = ("cells", "sub")
TILE = 256
VMEM_BYTES = 56 * 1024 * 1024


def shifted(value, axis, steps):
    count = lax.axis_size(axis)
    first, last = (max(0, -steps), min(count, count - steps))
    return lax.ppermute(value, axis, [(source, source + steps) for source in range(first, last)])


def ascend(children, upward_maps):
    width = children.shape[1]
    merged = children.reshape(-1, 8 * width)
    return jnp.dot(merged, upward_maps, preferred_element_type=jnp.float32).astype(jnp.bfloat16)


def gather_groups(table, base, index_ref, class_ref, picked, labels, grouped, kinds):
    width = table.shape[0]
    reach = table.shape[1]
    entries = index_ref.shape[0]
    tile = index_ref.shape[1]
    height = picked.shape[2]
    lower = height - width
    place = lax.broadcasted_iota(jnp.int32, (reach, tile), 0).astype(jnp.int16)
    blank = jnp.zeros((lower, tile), jnp.float32)
    classes = class_ref[...]
    for j in range(entries):
        index = (index_ref[j : j + 1, :] - base).astype(jnp.int16)
        hot = jnp.where(place == index, jnp.bfloat16(1), jnp.bfloat16(0))
        found = jnp.dot(table, hot, preferred_element_type=jnp.float32)
        picked[0, j] = jnp.concatenate([found, blank], axis=0).astype(jnp.bfloat16)
        picked[1, j] = jnp.concatenate([blank, found], axis=0).astype(jnp.bfloat16)
        wide = jnp.broadcast_to(classes[j : j + 1, :], (16, tile))
        labels[j] = wide.astype(jnp.int16)
    none = jnp.zeros((16, tile), jnp.bfloat16)
    for j in range(entries - 1, 0, -1):
        same = [labels[i] == labels[j] for i in range(j)]
        for side in range(2):
            for row in range(0, height, 16):
                total = picked[side, j, row : row + 16, :]
                for i in range(j):
                    total = total + jnp.where(same[i], picked[side, i, row : row + 16, :], none)
                picked[side, j, row : row + 16, :] = total

    def chosen(side, first, rows, wanted):
        found = [[none] * len(rows) for _ in wanted]
        for j in range(entries):
            match = [labels[j] == label for label in wanted]
            for r, row in enumerate(rows):
                piece = picked[side, j, row : row + 16, :]
                for k in range(len(wanted)):
                    found[k][r] = jnp.where(match[k], piece, found[k][r])
        return found

    pair = 2 * width
    span = 96
    body_rows = height - 16

    @pl.loop(0, kinds // 4)
    def _(step):
        kind = step * 4
        start = pl.multiple_of(step * (2 * pair), 16)
        wide = [jnp.full((16, tile), kind + k, jnp.int32).astype(jnp.int16) for k in range(4)]
        for side in range(2):
            wanted = [wide[side], wide[side + 2]]
            offset = side * (body_rows + 16)
            for at in range(0, body_rows, span):
                rows = list(range(at, min(at + span, body_rows), 16))
                found = chosen(side, at, [row + 16 * side for row in rows], wanted)
                for k in range(2):
                    for r, row in enumerate(rows):
                        grouped[pl.ds(start + (k * pair + offset + row), 16), :] = found[k][r]
        low = chosen(0, 0, [body_rows], [wide[0], wide[2]])
        high = chosen(1, 0, [0], [wide[1], wide[3]])
        for k in range(2):
            grouped[pl.ds(start + (k * pair + body_rows), 16), :] = low[k][0] + high[k][0]


def spread_kernel(block_ref, out_ref, held, send_sem, recv_sem):
    groups, members = held.shape[:2]
    group = lax.axis_index("cells")
    member = lax.axis_index("sub")
    near = [(group, lax.rem(member + k, members)) for k in range(1, members)]
    far = [(lax.rem(group + k, groups), member) for k in range(1, groups)]
    barrier = pltpu.get_barrier_semaphore()
    for device in near + far:
        pl.semaphore_signal(
            barrier, inc=1, device_id=device, device_id_type=pl.DeviceIdType.MESH
        )
    pl.semaphore_wait(barrier, len(near) + len(far))
    held[group, member] = block_ref[...]

    def exchange(view, devices, first):
        copies = [
            pltpu.make_async_remote_copy(
                src_ref=view,
                dst_ref=view,
                send_sem=send_sem.at[first + k],
                recv_sem=recv_sem.at[first + k],
                device_id=device,
                device_id_type=pl.DeviceIdType.MESH,
            )
            for k, device in enumerate(devices)
        ]
        for copy in copies:
            copy.start()
        for copy in copies:
            copy.wait()

    exchange(held.at[group, member], near, 0)
    exchange(held.at[group], far, len(near))
    out_ref[...] = held[...]


def spread(block):
    groups, members = lax.axis_size("cells"), lax.axis_size("sub")
    count, width = block.shape
    copies = groups + members - 2
    shape = (groups, members, count, width)
    held = pl.pallas_call(
        spread_kernel,
        out_shape=jax.ShapeDtypeStruct(shape, block.dtype),
        in_specs=[pl.BlockSpec(memory_space=pltpu.VMEM)],
        out_specs=pl.BlockSpec(memory_space=pltpu.VMEM),
        scratch_shapes=[
            pltpu.VMEM(shape, block.dtype),
            pltpu.SemaphoreType.DMA((copies,)),
            pltpu.SemaphoreType.DMA((copies,)),
        ],
        compiler_params=pltpu.CompilerParams(
            collective_id=0, has_side_effects=True, vmem_limit_bytes=VMEM_BYTES
        ),
    )(block)
    return held.reshape(-1, width)


def near_kernel(
    below_ref, own_ref, above_ref, index_ref, class_ref, maps_ref, out_ref, window, picked, labels, grouped, *, kinds
):
    step = pl.program_id(0)
    half = below_ref.shape[0]
    count = own_ref.shape[0]
    tile = index_ref.shape[1]
    reach = tile + 2 * half

    @pl.when(step == 0)
    def _():
        window[:, 0:half] = below_ref[...].T
        window[:, half : half + count] = own_ref[...].T
        window[:, half + count :] = above_ref[...].T

    first = pl.multiple_of(step * tile, tile)
    table = window[:, pl.ds(first, reach)]
    gather_groups(table, first, index_ref, class_ref, picked, labels, grouped, kinds)
    far = jnp.dot(maps_ref[...], grouped[...], preferred_element_type=jnp.float32)
    out_ref[...] = far.T


def near_far(below, own, above, index, classes, maps, kinds):
    count, width = own.shape
    half = below.shape[0]
    entries = index.shape[0]
    tile = min(count, TILE)
    total = maps.shape[1]
    height = (width + 15) // 16 * 16
    whole = lambda shape: pl.BlockSpec(shape, lambda i: (0, 0))
    return pl.pallas_call(
        functools.partial(near_kernel, kinds=kinds),
        grid=(count // tile,),
        in_specs=[
            whole(below.shape),
            whole(own.shape),
            whole(above.shape),
            pl.BlockSpec((entries, tile), lambda i: (0, i)),
            pl.BlockSpec((entries, tile), lambda i: (0, i)),
            whole(maps.shape),
        ],
        out_specs=pl.BlockSpec((tile, width), lambda i: (i, 0)),
        out_shape=jax.ShapeDtypeStruct((count, width), jnp.float32),
        scratch_shapes=[
            pltpu.VMEM((width, count + 2 * half), jnp.bfloat16),
            pltpu.VMEM((2, entries, height, tile), jnp.bfloat16),
            pltpu.VMEM((entries, 16, tile), jnp.int16),
            pltpu.VMEM((total, tile), jnp.bfloat16),
        ],
        compiler_params=pltpu.CompilerParams(vmem_limit_bytes=VMEM_BYTES),
        cost_estimate=pl.CostEstimate(
            flops=2 * count * width * (total + entries * (tile + 2 * half)),
            bytes_accessed=2 * width * total,
            transcendentals=0,
        ),
    )(below, own, above, index, classes, maps)


def far_kernel(
    table_ref, index_ref, class_ref, maps_ref, down_ref, near_ref, out_ref,
    picked, labels, grouped, far, local_five, local_six, local_seven, *, kinds, counts
):
    count_six, count_five, count_four = counts
    gather_groups(table_ref[...], 0, index_ref, class_ref, picked, labels, grouped, kinds)
    far[...] = jnp.dot(maps_ref[...], grouped[...], preferred_element_type=jnp.float32).T
    start_four = count_six + count_five

    def descend(parents, local):
        for octant in range(8):
            spread = jnp.dot(parents, down_ref[octant], preferred_element_type=jnp.float32)
            local[:, octant, :] = spread[: local.shape[0]]
        count, _, width = local.shape
        return local[...].reshape(8 * count, width)

    rows_four = far[start_four : start_four + 16, :].astype(jnp.bfloat16)
    five = descend(rows_four, local_five) + far[count_six:start_four, :]
    six = descend(five.astype(jnp.bfloat16), local_six) + far[0:count_six, :]
    seven = descend(six.astype(jnp.bfloat16), local_seven) + near_ref[...]
    out_ref[...] = seven.astype(jnp.bfloat16)


def coarse_far(table, index, classes, maps, down, near, kinds, counts):
    width = table.shape[0]
    entries, tile = index.shape
    total = maps.shape[1]
    height = (width + 15) // 16 * 16
    return pl.pallas_call(
        functools.partial(far_kernel, kinds=kinds, counts=counts),
        out_shape=jax.ShapeDtypeStruct(near.shape, jnp.bfloat16),
        scratch_shapes=[
            pltpu.VMEM((2, entries, height, tile), jnp.bfloat16),
            pltpu.VMEM((entries, 16, tile), jnp.int16),
            pltpu.VMEM((total, tile), jnp.bfloat16),
            pltpu.VMEM((tile, width), jnp.float32),
            pltpu.VMEM((counts[2], 8, width), jnp.float32),
            pltpu.VMEM((counts[1], 8, width), jnp.float32),
            pltpu.VMEM((counts[0], 8, width), jnp.float32),
        ],
        compiler_params=pltpu.CompilerParams(vmem_limit_bytes=VMEM_BYTES),
        cost_estimate=pl.CostEstimate(
            flops=2 * tile * width * total, bytes_accessed=2 * width * total, transcendentals=0
        ),
    )(table, index, classes, maps, down, near)


def body(
    leaf_multipoles,
    occupancy,
    upward_maps,
    transfer_maps,
    downward_maps,
    sources_seven,
    classes_seven,
    sources_six,
    classes_six,
    sources_five,
    classes_five,
    sources_four,
    classes_four,
):
    width = leaf_multipoles.shape[1]
    kinds = transfer_maps.shape[0] // width
    place = lax.axis_index(AXES)
    count_seven = sources_seven.shape[0]
    count_six = sources_six.shape[0]
    count_five = sources_five.shape[0]
    count_four = sources_four.shape[0]
    half = count_seven // 2

    multi_seven = jnp.where(
        occupancy[:, None] > 0, leaf_multipoles, jnp.zeros_like(leaf_multipoles)
    )
    below = shifted(multi_seven[-half:], AXES, 1)
    above = shifted(multi_seven[:half], AXES, -1)
    multi_six = ascend(multi_seven, upward_maps)
    multi_five = ascend(multi_six, upward_maps)
    table_five = spread(multi_five)

    maps = transfer_maps.T
    down = downward_maps.reshape(width, 8, width).transpose(1, 0, 2)

    index_seven = (sources_seven - (place * count_seven - half)).T
    near = near_far(below, multi_seven, above, index_seven, classes_seven.T, maps, kinds)

    edges = ascend(jnp.concatenate([below, above], axis=0), upward_maps)
    reach = half // 8
    table_four = ascend(table_five, upward_maps)
    table = jnp.concatenate(
        [edges[:reach], multi_six, edges[reach:], table_five, table_four], axis=0
    )
    start_five = count_six + 2 * reach
    start_four = start_five + table_five.shape[0]
    rest = (-table.shape[0]) % 128
    table = jnp.pad(table, ((0, rest), (0, 0)))
    used = count_six + count_five + count_four
    tile = (used + 16 + 127) // 128 * 128
    index = jnp.concatenate(
        [
            sources_six - (place * count_six - reach),
            sources_five + start_five,
            sources_four + start_four,
        ],
        axis=0,
    )
    index = jnp.pad(index, ((0, tile - used), (0, 0)))
    classes = jnp.concatenate([classes_six, classes_five, classes_four], axis=0)
    classes = jnp.pad(classes, ((0, tile - used), (0, 0)), constant_values=kinds)
    return coarse_far(
        table.T, index.T, classes.T, maps, down, near, kinds, (count_six, count_five, count_four)
    )


def solution(mesh):
    row = P(AXES, None)
    in_specs = (row, P(AXES), P(), P(), P()) + (row,) * 8
    return jax.shard_map(body, mesh=mesh, in_specs=in_specs, out_specs=row, check_vma=False)
```

```python
import functools

import jax
import jax.numpy as jnp
from jax import lax
from jax.experimental import pallas as pl
from jax.experimental.pallas import tpu as pltpu
from jax.sharding import PartitionSpec as P

AXES = ("cells", "sub")
TILE = 512
VMEM_BYTES = 56 * 1024 * 1024


def shifted(value, axis, steps):
    count = lax.axis_size(axis)
    first, last = (max(0, -steps), min(count, count - steps))
    return lax.ppermute(value, axis, [(source, source + steps) for source in range(first, last)])


def ascend(children, upward_maps):
    width = children.shape[1]
    merged = children.reshape(-1, 8 * width)
    return jnp.dot(merged, upward_maps, preferred_element_type=jnp.float32).astype(jnp.bfloat16)


def gather_groups(table, base, index_ref, class_ref, picked, labels, grouped, kinds):
    width = table.shape[0]
    reach = table.shape[1]
    entries = index_ref.shape[0]
    tile = index_ref.shape[1]
    height = picked.shape[2]
    lower = height - width
    place = lax.broadcasted_iota(jnp.int32, (reach, tile), 0).astype(jnp.int16)
    blank = jnp.zeros((lower, tile), jnp.float32)
    classes = class_ref[...]
    for j in range(0, entries, 2):
        hots = []
        for i in (j, j + 1):
            index = (index_ref[i : i + 1, :] - base).astype(jnp.int16)
            hots.append(jnp.where(place == index, jnp.bfloat16(1), jnp.bfloat16(0)))
        both = jnp.dot(table, jnp.concatenate(hots, axis=1), preferred_element_type=jnp.float32)
        for i in (j, j + 1):
            found = both[:, (i - j) * tile : (i - j + 1) * tile]
            picked[0, i] = jnp.concatenate([found, blank], axis=0).astype(jnp.bfloat16)
            picked[1, i] = jnp.concatenate([blank, found], axis=0).astype(jnp.bfloat16)
    for j in range(entries):
        wide = jnp.broadcast_to(classes[j : j + 1, :], (16, tile))
        labels[j] = wide.astype(jnp.int16)
    none = jnp.zeros((16, tile), jnp.bfloat16)
    for j in range(entries - 1, 0, -1):
        same = [labels[i] == labels[j] for i in range(j)]
        for side in range(2):
            for row in range(0, height, 16):
                total = picked[side, j, row : row + 16, :]
                for i in range(j):
                    total = total + jnp.where(same[i], picked[side, i, row : row + 16, :], none)
                picked[side, j, row : row + 16, :] = total

    def chosen(side, first, rows, wanted):
        found = [[none] * len(rows) for _ in wanted]
        for j in range(entries):
            match = [labels[j] == label for label in wanted]
            for r, row in enumerate(rows):
                piece = picked[side, j, row : row + 16, :]
                for k in range(len(wanted)):
                    found[k][r] = jnp.where(match[k], piece, found[k][r])
        return found

    pair = 2 * width
    span = max(16, 96 * 256 // tile // 16 * 16)
    body_rows = height - 16

    @pl.loop(0, kinds // 4)
    def _(step):
        kind = step * 4
        start = pl.multiple_of(step * (2 * pair), 16)
        wide = [jnp.full((16, tile), kind + k, jnp.int32).astype(jnp.int16) for k in range(4)]
        for side in range(2):
            wanted = [wide[side], wide[side + 2]]
            offset = side * (body_rows + 16)
            for at in range(0, body_rows, span):
                rows = list(range(at, min(at + span, body_rows), 16))
                found = chosen(side, at, [row + 16 * side for row in rows], wanted)
                for k in range(2):
                    for r, row in enumerate(rows):
                        grouped[pl.ds(start + (k * pair + offset + row), 16), :] = found[k][r]
        low = chosen(0, 0, [body_rows], [wide[0], wide[2]])
        high = chosen(1, 0, [0], [wide[1], wide[3]])
        for k in range(2):
            grouped[pl.ds(start + (k * pair + body_rows), 16), :] = low[k][0] + high[k][0]


def spread_kernel(block_ref, out_ref, held, send_sem, recv_sem):
    groups, members = held.shape[:2]
    group = lax.axis_index("cells")
    member = lax.axis_index("sub")
    near = [(group, lax.rem(member + k, members)) for k in range(1, members)]
    far = [(lax.rem(group + k, groups), member) for k in range(1, groups)]
    barrier = pltpu.get_barrier_semaphore()
    for device in near + far:
        pl.semaphore_signal(
            barrier, inc=1, device_id=device, device_id_type=pl.DeviceIdType.MESH
        )
    pl.semaphore_wait(barrier, len(near) + len(far))
    held[group, member] = block_ref[...]

    def exchange(view, devices, first):
        copies = [
            pltpu.make_async_remote_copy(
                src_ref=view,
                dst_ref=view,
                send_sem=send_sem.at[first + k],
                recv_sem=recv_sem.at[first + k],
                device_id=device,
                device_id_type=pl.DeviceIdType.MESH,
            )
            for k, device in enumerate(devices)
        ]
        for copy in copies:
            copy.start()
        for copy in copies:
            copy.wait()

    exchange(held.at[group, member], near, 0)
    exchange(held.at[group], far, len(near))
    out_ref[...] = held[...]


def spread(block):
    groups, members = lax.axis_size("cells"), lax.axis_size("sub")
    count, width = block.shape
    copies = groups + members - 2
    shape = (groups, members, count, width)
    held = pl.pallas_call(
        spread_kernel,
        out_shape=jax.ShapeDtypeStruct(shape, block.dtype),
        in_specs=[pl.BlockSpec(memory_space=pltpu.VMEM)],
        out_specs=pl.BlockSpec(memory_space=pltpu.VMEM),
        scratch_shapes=[
            pltpu.VMEM(shape, block.dtype),
            pltpu.SemaphoreType.DMA((copies,)),
            pltpu.SemaphoreType.DMA((copies,)),
        ],
        compiler_params=pltpu.CompilerParams(
            collective_id=0, has_side_effects=True, vmem_limit_bytes=VMEM_BYTES
        ),
    )(block)
    return held.reshape(-1, width)


def near_kernel(
    below_ref, own_ref, above_ref, index_ref, class_ref, maps_ref, out_ref, window, picked, labels, grouped, *, kinds
):
    step = pl.program_id(0)
    half = below_ref.shape[0]
    count = own_ref.shape[0]
    tile = index_ref.shape[1]
    reach = tile + 2 * half

    @pl.when(step == 0)
    def _():
        window[:, 0:half] = below_ref[...].T
        window[:, half : half + count] = own_ref[...].T
        window[:, half + count :] = above_ref[...].T

    first = pl.multiple_of(step * tile, tile)
    table = window[:, pl.ds(first, reach)]
    gather_groups(table, first, index_ref, class_ref, picked, labels, grouped, kinds)
    out_ref[...] = jnp.dot(maps_ref[...], grouped[...], preferred_element_type=jnp.float32)


def near_far(below, own, above, index, classes, maps, kinds):
    count, width = own.shape
    half = below.shape[0]
    entries = index.shape[0]
    tile = min(count, TILE)
    total = maps.shape[1]
    height = (width + 15) // 16 * 16
    whole = lambda shape: pl.BlockSpec(shape, lambda i: (0, 0))
    return pl.pallas_call(
        functools.partial(near_kernel, kinds=kinds),
        grid=(count // tile,),
        in_specs=[
            whole(below.shape),
            whole(own.shape),
            whole(above.shape),
            pl.BlockSpec((entries, tile), lambda i: (0, i)),
            pl.BlockSpec((entries, tile), lambda i: (0, i)),
            whole(maps.shape),
        ],
        out_specs=pl.BlockSpec((width, tile), lambda i: (0, i)),
        out_shape=jax.ShapeDtypeStruct((width, count), jnp.float32),
        scratch_shapes=[
            pltpu.VMEM((width, count + 2 * half), jnp.bfloat16),
            pltpu.VMEM((2, entries, height, tile), jnp.bfloat16),
            pltpu.VMEM((entries, 16, tile), jnp.int16),
            pltpu.VMEM((total, tile), jnp.bfloat16),
        ],
        compiler_params=pltpu.CompilerParams(vmem_limit_bytes=VMEM_BYTES),
        cost_estimate=pl.CostEstimate(
            flops=2 * count * width * (total + entries * (tile + 2 * half)),
            bytes_accessed=2 * width * total,
            transcendentals=0,
        ),
    )(below, own, above, index, classes, maps)


def far_kernel(
    table_ref, index_ref, class_ref, maps_ref, down_ref, near_ref, out_ref,
    picked, labels, grouped, far, local_five, local_six, local_seven, *, kinds, counts
):
    count_six, count_five, count_four = counts
    gather_groups(table_ref[...], 0, index_ref, class_ref, picked, labels, grouped, kinds)
    far[...] = jnp.dot(maps_ref[...], grouped[...], preferred_element_type=jnp.float32).T
    start_four = count_six + count_five

    def descend(parents, local):
        count, _, width = local.shape
        wide = jnp.dot(parents, down_ref[...], preferred_element_type=jnp.float32)
        for octant in range(8):
            local[:, octant, :] = wide[:count, octant * width : (octant + 1) * width]
        return local[...].reshape(8 * count, width)

    rows_four = far[start_four : start_four + 16, :].astype(jnp.bfloat16)
    five = descend(rows_four, local_five) + far[count_six:start_four, :]
    six = descend(five.astype(jnp.bfloat16), local_six) + far[0:count_six, :]
    seven = descend(six.astype(jnp.bfloat16), local_seven)
    out_ref[...] = (seven.T + near_ref[...]).astype(jnp.bfloat16)


def coarse_far(table, index, classes, maps, down, near, kinds, counts):
    width = table.shape[0]
    entries, tile = index.shape
    total = maps.shape[1]
    height = (width + 15) // 16 * 16
    return pl.pallas_call(
        functools.partial(far_kernel, kinds=kinds, counts=counts),
        out_shape=jax.ShapeDtypeStruct(near.shape, jnp.bfloat16),
        scratch_shapes=[
            pltpu.VMEM((2, entries, height, tile), jnp.bfloat16),
            pltpu.VMEM((entries, 16, tile), jnp.int16),
            pltpu.VMEM((total, tile), jnp.bfloat16),
            pltpu.VMEM((tile, width), jnp.float32),
            pltpu.VMEM((counts[2], 8, width), jnp.float32),
            pltpu.VMEM((counts[1], 8, width), jnp.float32),
            pltpu.VMEM((counts[0], 8, width), jnp.float32),
        ],
        compiler_params=pltpu.CompilerParams(vmem_limit_bytes=VMEM_BYTES),
        cost_estimate=pl.CostEstimate(
            flops=2 * tile * width * total, bytes_accessed=2 * width * total, transcendentals=0
        ),
    )(table, index, classes, maps, down, near)


def body(
    leaf_multipoles,
    occupancy,
    upward_maps,
    transfer_maps,
    downward_maps,
    sources_seven,
    classes_seven,
    sources_six,
    classes_six,
    sources_five,
    classes_five,
    sources_four,
    classes_four,
):
    width = leaf_multipoles.shape[1]
    kinds = transfer_maps.shape[0] // width
    place = lax.axis_index(AXES)
    count_seven = sources_seven.shape[0]
    count_six = sources_six.shape[0]
    count_five = sources_five.shape[0]
    count_four = sources_four.shape[0]
    half = count_seven // 2

    multi_seven = jnp.where(
        occupancy[:, None] > 0, leaf_multipoles, jnp.zeros_like(leaf_multipoles)
    )
    below = shifted(multi_seven[-half:], AXES, 1)
    above = shifted(multi_seven[:half], AXES, -1)
    multi_six = ascend(multi_seven, upward_maps)
    multi_five = ascend(multi_six, upward_maps)
    table_five = spread(multi_five)

    maps = transfer_maps.T

    index_seven = (sources_seven - (place * count_seven - half)).T
    near = near_far(below, multi_seven, above, index_seven, classes_seven.T, maps, kinds)

    edges = ascend(jnp.concatenate([below, above], axis=0), upward_maps)
    reach = half // 8
    table_four = ascend(table_five, upward_maps)
    table = jnp.concatenate(
        [edges[:reach], multi_six, edges[reach:], table_five, table_four], axis=0
    )
    start_five = count_six + 2 * reach
    start_four = start_five + table_five.shape[0]
    rest = (-table.shape[0]) % 128
    table = jnp.pad(table, ((0, rest), (0, 0)))
    used = count_six + count_five + count_four
    tile = (used + 16 + 127) // 128 * 128
    index = jnp.concatenate(
        [
            sources_six - (place * count_six - reach),
            sources_five + start_five,
            sources_four + start_four,
        ],
        axis=0,
    )
    index = jnp.pad(index, ((0, tile - used), (0, 0)))
    classes = jnp.concatenate([classes_six, classes_five, classes_four], axis=0)
    classes = jnp.pad(classes, ((0, tile - used), (0, 0)), constant_values=kinds)
    return coarse_far(
        table.T, index.T, classes.T, maps, downward_maps, near, kinds,
        (count_six, count_five, count_four),
    ).T


def solution(mesh):
    row = P(AXES, None)
    in_specs = (row, P(AXES), P(), P(), P()) + (row,) * 8
    return jax.shard_map(body, mesh=mesh, in_specs=in_specs, out_specs=row, check_vma=False)
```
